512 devices in a mesh: occ: 16 (over y_lo, x, core), vir: 32 (over z, y_hi).
Axes of the slice: x: 4, y: 4 (y_hi: 2, y_lo: 2; y = y_hi * 2 + y_lo), z: 16, core: 2. Of those that a mesh axis runs over, the one named last changes fastest.
Arguments:
- factor: float32 [16, 4096, 1280], P('occ', 'vir'), may hold values from -0.6 to 0.6
- occ_energy: float32 [16], P('occ'), may hold values from -2 to -0.5
- vir_energy: float32 [4096], P('vir'), may hold values from 0.2 to 4.7
Outputs:
- aux_density: float32 [16, 4096, 1280], P('occ', 'vir')
- pair_trace: float32 [16, 3], P('occ')
The draws below stay inside these ranges and needn't reach their ends.
All inputs are finite; a program needn't handle non-finite values.
Results may differ from the reference program's by a relative error of at most 0.00013.
Values sent between devices are 32-bit elements; how exact they have to be, the bound alone decides.
A program may use at most 64 MiB of HBM per device.

```python
import math
import jax
import jax.numpy as jnp
from jax import lax

NVIR = 4096
NAUX = 1280
OCC_DEV = 1
STEPS = 3
NOCC = 16
N_OCC = 16
N_VIR = 32


def draw_vir_energy(key, part):
    position = jnp.arange(NVIR, dtype=jnp.float32) / NVIR
    spread = jnp.exp(jax.random.uniform(key, (NVIR,), jnp.float32, math.log(0.7), math.log(1.4)))
    return (0.3 + 3.0 * position) * spread


def shard_levels(stream_key, extent, split, smallest, top_value):
    level, own = 1.0, jax.random.fold_in(stream_key, 6)
    for axis_at, shards_of in split:
        heights = jnp.exp(jax.random.uniform(jax.random.fold_in(own, axis_at), (shards_of,), jnp.float32, smallest / len(split), top_value / len(split)))
        level = level * jnp.repeat(heights, extent[axis_at] // shards_of).reshape([-1 if axis == axis_at else 1 for axis in range(len(extent))])
    return level


def bell_draw(key, shape, width, reach, split=(), kind=jnp.bfloat16):
    entries = jax.random.normal(key, shape, jnp.float32) * width
    if len(split) > 0:
        entries = shard_levels(key, shape, split, -0.22, 0.18) * entries
    return jnp.clip(entries, min=-reach, max=reach).astype(kind)


def setup_inputs(seed: int = 0) -> dict:
    key_list = jax.random.split(jax.random.key(seed), 4)
    factor = bell_draw(key_list[0], (NOCC, NVIR, NAUX), 0.09, 0.6, ((0, 16), (1, 32)), jnp.float32)
    occ_energy = jnp.clip(-2.0 + 1.5 * jax.random.uniform(key_list[1], (NOCC,), jnp.float32) ** shard_levels(key_list[1], (NOCC,), ((0, 16),), -0.2, 0.2), -2.0, -0.5)
    vir_energy = draw_vir_energy(jax.random.fold_in(key_list[3], 71), 0)
    return {"factor": factor, "occ_energy": occ_energy, "vir_energy": vir_energy}


def contract(pattern, former, latter):
    return jnp.einsum(pattern, former, latter, precision=lax.Precision.HIGHEST, preferred_element_type=jnp.float32)


def flip_pairs(tensor, dim_index):
    old_shape = tensor.shape
    new_shape = old_shape[:dim_index] + (old_shape[dim_index] // 2, 2) + old_shape[dim_index + 1:]
    return jnp.flip(tensor.reshape(new_shape), dim_index + 1).reshape(old_shape)


def reference(factor, occ_energy, vir_energy):
    vir_dev = NVIR // N_VIR
    occ_blocks = factor.reshape(N_OCC, OCC_DEV, N_VIR, vir_dev, NAUX)
    occ_levels = occ_energy.reshape(N_OCC, OCC_DEV)
    vir_levels = vir_energy.reshape(N_VIR, vir_dev)
    vir_far = flip_pairs(vir_levels, 0)
    density = jnp.zeros(occ_blocks.shape, jnp.float32)
    traces = []
    for offset in range(STEPS):
        cycle_rows = jnp.roll(occ_blocks, offset, axis=0)
        cycle_occ = jnp.roll(occ_levels, offset, axis=0)
        far_rows = flip_pairs(cycle_rows, 2)
        pair_occ = occ_levels[:, :, None] + cycle_occ[:, None, :]
        gap_diag = pair_occ[:, :, :, None, None, None] - vir_levels[None, None, None, :, :, None] - vir_levels[None, None, None, :, None, :]
        gap_off = pair_occ[:, :, :, None, None, None] - vir_levels[None, None, None, :, :, None] - vir_far[None, None, None, :, None, :]
        k_diag = contract("oivap,ojvbp->oijvab", occ_blocks, cycle_rows)
        k_off = contract("oivap,ojvbp->oijvab", occ_blocks, far_rows)
        amp_diag = k_diag / gap_diag
        amp_off = k_off / gap_off
        bar_diag = 2.0 * amp_diag - jnp.swapaxes(amp_diag, 4, 5)
        k_cross = jnp.swapaxes(flip_pairs(k_off, 3), 4, 5)
        bar_off = 2.0 * amp_off - k_cross / gap_off
        traces.append(jnp.sum(amp_diag * bar_diag + amp_off * bar_off, axis=(3, 4, 5)) / NVIR)
        density = density + contract("oijvab,ojvbp->oivap", bar_diag, cycle_rows) + contract("oijvab,ojvbp->oivap", bar_off, far_rows)
        returned = contract("oijvab,oivap->ojvbp", bar_diag, occ_blocks) + flip_pairs(contract("oijvab,oivap->ojvbp", bar_off, occ_blocks), 2)
        density = density + jnp.roll(returned, -offset, axis=0)
    pair_trace = jnp.stack(traces, axis=2).reshape(N_OCC * OCC_DEV, STEPS * OCC_DEV)
    return density.reshape(N_OCC * OCC_DEV, NVIR, NAUX), pair_trace
```

```python
import jax
import jax.numpy as jnp
from jax import lax
from jax.experimental import pallas as pl
from jax.experimental.pallas import tpu as pltpu
from jax.sharding import PartitionSpec as P

NVIR = 4096
NAUX = 1280
ROWS = 128
NCH = 4
CH = ROWS // NCH
COLS = 256
MESH = pl.DeviceIdType.MESH
F32 = jnp.float32
BF16 = jnp.bfloat16

OWN, SIB, UP, DOWN, REST = range(5)
(
    S_SIB, S_UP, S_DOWN, S_PART, S_REST, S_FAR_UP, S_FAR_DOWN, S_FAR_SIB, S_FAR_REST,
    S_WRAP, S_CROSS,
) = range(11)


def halves(value):
    high = value.astype(BF16)
    return high, (value - high.astype(F32)).astype(BF16)


def rows_dot(former, latter):
    dims = (((1,), (1,)), ((), ()))

    def dot(a, b):
        return lax.dot_general(a, b, dims, preferred_element_type=F32)

    return dot(former[0], latter[0]) + (dot(former[0], latter[1]) + dot(former[1], latter[0]))


def folded(tile):
    return jnp.sum(tile.reshape(tile.shape[0] // 8, 8, 128), axis=0)


def kernel(
    factor, occ, vir, density, trace,
    own, near, far, staged, near_h, near_l, far_h, far_l, crossed, energy, energies, sums,
    tile_out, tile_in, next_out, next_in,
    own_sem, send_sem, near_sem, far_sem, staged_sem, e_send, e_recv, t_send, t_recv,
):
    o = lax.axis_index("occ")
    v = lax.axis_index("vir")
    q = lax.rem(o, 2)
    x = lax.rem(o // 2, 4)
    y_lo = o // 8
    other_row = o + 8 - 16 * y_lo
    sibling = o + 1 - 2 * q
    mate = v + 1 - 2 * lax.rem(v, 2)
    first = x == 0
    last = x == 3
    edge = jnp.logical_or(first, last)
    inner = jnp.logical_not(edge)
    across = jnp.where(last, o - 6, o + 6)

    def occ_at(distance):
        return lax.rem(o + distance + 16, 16)

    up, down = occ_at(2), occ_at(-2)
    beyond = jnp.where(last, up, down)

    def flipped(r):
        z = v
        out = v
        for bit in (1, 2, 4, 8, 16):
            if r & bit:
                out = out + bit - 2 * bit * lax.rem(z // bit, 2)
        return out

    own_copy = pltpu.make_async_copy(factor.at[0], own, own_sem)
    own_copy.start()

    barrier = pltpu.get_barrier_semaphore()
    peers = [(occ_at(d), v) for d in (1, -1, 2, -2)]
    peers += [(o, flipped(r)) for r in (1, 2, 3, 4, 5, 6, 7, 8, 16, 24)]
    for peer in peers:
        pl.semaphore_signal(barrier, inc=1, device_id=peer, device_id_type=MESH)

    @pl.when(edge)
    def _():
        for peer in ((other_row, v), (across, v), (other_row, mate), (beyond, mate)):
            pl.semaphore_signal(barrier, inc=1, device_id=peer, device_id_type=MESH)

    energy[...] = jnp.zeros((8, 128), F32)
    energy[0:1, :] = vir[...]
    energy[1:2, :] = jnp.broadcast_to(occ[...], (1, 128))

    pl.semaphore_wait(barrier, jnp.where(edge, len(peers) + 4, len(peers)))

    def remote(src, dst, send, recv, device):
        return pltpu.make_async_remote_copy(
            src_ref=src, dst_ref=dst, send_sem=send, recv_sem=recv,
            device_id=device, device_id_type=MESH,
        )

    def part(ref, n):
        return ref.at[pl.ds(n * CH, CH)]

    def mine(n):
        return factor.at[0, pl.ds(n * CH, CH)]

    def to_near(src, slot, n, flow, device):
        return remote(
            src, near.at[slot, pl.ds(n * CH, CH)], send_sem.at[flow, n], near_sem.at[slot, n], device
        )

    def to_far(src, slot, n, flow, device):
        return remote(
            src, far.at[slot, pl.ds(n * CH, CH)], send_sem.at[flow, n], far_sem.at[slot, n], device
        )

    def to_staged(n):
        return remote(
            mine(n), part(staged, n), send_sem.at[S_PART, n], staged_sem.at[n], (other_row, v)
        )

    def near_part(slot, n):
        return near.at[slot, pl.ds(n * CH, CH)]

    def far_part(slot, n):
        return far.at[slot, pl.ds(n * CH, CH)]

    def sib_side(slot, n):
        return slot

    e_peers = [(occ_at(1), v), (occ_at(-1), v), (occ_at(2), v), (occ_at(-2), v), (o, mate)]
    e_copies = [
        remote(energy, energies.at[k], e_send.at[k], e_recv.at[k], peer)
        for k, peer in enumerate(e_peers)
    ]
    for copy in e_copies:
        copy.start()

    for n in range(NCH):
        @pl.when(edge)
        def _():
            to_staged(n).start()

        @pl.when(inner)
        def _():
            to_far(mine(n), 0, n, S_PART, (o, mate)).start()

        @pl.when(jnp.logical_not(last))
        def _():
            to_near(mine(n), DOWN, n, S_UP, (up, v)).start()

        @pl.when(jnp.logical_not(first))
        def _():
            to_near(mine(n), UP, n, S_DOWN, (down, v)).start()

        to_near(mine(n), SIB, n, S_SIB, (sibling, v)).start()

    def wait_near(slot, n):
        to_near(near_part(slot, n), slot, n, S_SIB, (sibling, v)).wait_recv()

    def wait_far(slot, n):
        to_far(far_part(slot, n), slot, n, S_SIB, (sibling, v)).wait_recv()

    def relay_staged(n):
        @pl.when(edge)
        def _():
            to_staged(n).wait_recv()
            to_near(part(staged, n), jnp.where(last, DOWN, UP), n, S_WRAP, (across, v)).start()
            to_far(part(staged, n), 0, n, S_CROSS, (other_row, mate)).start()

    def relay_partner(n):
        wait_far(0, n)

        @pl.when(jnp.logical_not(last))
        def _():
            to_far(far_part(0, n), DOWN, n, S_FAR_UP, (up, v)).start()

        @pl.when(last)
        def _():
            to_far(mine(n), DOWN, n, S_FAR_UP, (up, mate)).start()

        @pl.when(jnp.logical_not(first))
        def _():
            to_far(far_part(0, n), UP, n, S_FAR_DOWN, (down, v)).start()

        @pl.when(first)
        def _():
            to_far(mine(n), UP, n, S_FAR_DOWN, (down, mate)).start()

        to_far(far_part(0, n), SIB, n, S_FAR_SIB, (sibling, v)).start()

    passed = jnp.where(q == 0, UP, DOWN)

    def relay_near(n):
        wait_near(UP, n)
        wait_near(DOWN, n)
        to_near(near_part(passed, n), REST, n, S_REST, (sibling, v)).start()

    def relay_far(n):
        wait_far(UP, n)
        wait_far(DOWN, n)
        to_far(far_part(passed, n), REST, n, S_FAR_REST, (sibling, v)).start()

    def split_near(slot, start, count):
        rows = pl.ds(slot * ROWS + start, count)
        h, l = halves(near[slot, pl.ds(start, count), :])
        near_h[rows, :] = h
        near_l[rows, :] = l

    def split_far(slot, start, count):
        rows = pl.ds(slot * ROWS + start, count)
        h, l = halves(far[slot, pl.ds(start, count), :])
        far_h[rows, :] = h
        far_l[rows, :] = l

    def near_rows(slot, count=1):
        rows = pl.ds(slot * ROWS, count * ROWS)
        return near_h[rows, :], near_l[rows, :]

    def add_density(weights, latter_h, latter_l, fresh=False):
        w_h, w_l = halves(weights)
        for c in range(NAUX // COLS):
            cols = pl.ds(c * COLS, COLS)
            h, l = latter_h[:, cols], latter_l[:, cols]
            term = (
                jnp.dot(w_h, h, preferred_element_type=F32)
                + jnp.dot(w_h, l, preferred_element_type=F32)
                + jnp.dot(w_l, h, preferred_element_type=F32)
            )
            density[0, :, cols] = term if fresh else density[0, :, cols] + term

    def pair_energy(slot):
        if slot == OWN:
            row = energy[1:2, :]
        elif slot == UP:
            row = energies[3, 1:2, :]
        elif slot == DOWN:
            row = energies[2, 1:2, :]
        elif slot == SIB:
            row = jnp.where(q == 0, energies[1, 1:2, :], energies[0, 1:2, :])
        else:
            row = jnp.where(q == 0, energies[0, 1:2, :], energies[1, 1:2, :])
        return row + energy[1:2, :]

    def diag_weights(k_tile, slot):
        across_b = jnp.broadcast_to(energy[0:1, :], (ROWS, 128))
        gap = pair_energy(slot) - across_b.T - across_b
        amp = k_tile / gap
        bar = 2.0 * amp - amp.T
        sums[slot] = folded(amp * bar)
        return 2.0 * bar if slot == OWN else bar

    relay_staged(0)
    own_copy.wait()
    h, l = halves(own[...])
    near_h[0:ROWS, :] = h
    near_l[0:ROWS, :] = l
    for copy in e_copies:
        copy.wait()
    for n in range(NCH):
        wait_near(SIB, n)
    split_near(SIB, 0, ROWS)
    k_first = rows_dot(near_rows(OWN), near_rows(OWN, 2))
    bars = jnp.concatenate(
        [diag_weights(k_first[:, :128], OWN), diag_weights(k_first[:, 128:], SIB)], axis=1
    )
    add_density(bars, near_h.at[0:256], near_l.at[0:256], fresh=True)

    for n in range(1, NCH + 1):
        if n < NCH:
            relay_staged(n)
        relay_partner(n - 1)
        relay_near(n - 1)
        start = (n - 1) * CH
        split_far(0, start, CH)
        split_near(UP, start, CH)
        split_near(DOWN, start, CH)

    k_next = rows_dot(near_rows(OWN), near_rows(UP, 2))
    bars = jnp.concatenate(
        [diag_weights(k_next[:, :128], UP), diag_weights(k_next[:, 128:], DOWN)], axis=1
    )
    add_density(bars, near_h.at[256:512], near_l.at[256:512])
    for n in range(NCH):
        wait_near(REST, n)
    split_near(REST, 0, ROWS)
    k_rest = rows_dot(near_rows(OWN), near_rows(REST))
    add_density(diag_weights(k_rest, REST), near_h.at[512:640], near_l.at[512:640])

    far_row = jnp.broadcast_to(energies[4, 0:1, :], (ROWS, 128)).T
    own_row = jnp.broadcast_to(energy[0:1, :], (ROWS, 128))
    partner = (far_h[0:ROWS, :], far_l[0:ROWS, :])
    for slot in range(5):
        k_tile = rows_dot(partner, near_rows(slot))
        crossed[slot] = k_tile / (pair_energy(slot) - far_row - own_row)
    weights = crossed[OWN]
    sums[OWN] += folded(weights * weights)
    add_density(2.0 * weights.T, far_h.at[0:ROWS], far_l.at[0:ROWS])

    mix_h, mix_l = tile_h, tile_l = None, None
    own_pair = near_rows(OWN)
    for n in range(NCH):
        relay_far(n)
        start = n * CH
        wait_far(SIB, n)
        wait_far(REST, n)
        pieces = [halves(far[slot, pl.ds(start, CH), :]) for slot in (SIB, UP, DOWN, REST)]
        lot_h = jnp.concatenate([p[0] for p in pieces], axis=0)
        lot_l = jnp.concatenate([p[1] for p in pieces], axis=0)
        far_h[0:4 * CH, :] = lot_h
        far_l[0:4 * CH, :] = lot_l
        k_tile = rows_dot((far_h[0:4 * CH, :], far_l[0:4 * CH, :]), own_pair)
        bars = []
        side = far_row[start:start + CH, :]
        for at, slot in enumerate((SIB, UP, DOWN, REST)):
            gap = pair_energy(slot) - side - own_row[0:CH, :]
            amp = k_tile[at * CH:(at + 1) * CH, :] / gap
            bar = 2.0 * amp - crossed[slot, pl.ds(start, CH), :]
            sums[slot] += folded(amp * bar)
            bars.append(bar)
        weights = jnp.concatenate(bars, axis=0).T
        if n == NCH - 1:
            before = jnp.where(q == 0, sums[REST], sums[SIB])
            tile_out[...] = jnp.zeros((8, 128), F32)
            tile_out[0:1, :] = jnp.sum(sums[OWN], axis=0, keepdims=True)
            tile_out[1:2, :] = jnp.sum(before, axis=0, keepdims=True)
            tile_out[2:3, :] = jnp.sum(sums[DOWN], axis=0, keepdims=True)
            round_one = [
                remote(tile_out, tile_in.at[r - 1], t_send.at[r - 1], t_recv.at[r - 1], (o, flipped(r)))
                for r in range(1, 8)
            ]
            for copy in round_one:
                copy.start()
        add_density(weights, far_h.at[0:4 * CH], far_l.at[0:4 * CH])

    total = tile_out[...]
    for copy in round_one:
        copy.wait_recv()
    for r in range(7):
        total = total + tile_in[r]
    next_out[...] = total
    round_two = [
        remote(next_out, next_in.at[k], t_send.at[7 + k], t_recv.at[7 + k], (o, flipped(r)))
        for k, r in enumerate((8, 16, 24))
    ]
    for copy in round_two:
        copy.start()
    for copy in round_one:
        copy.wait_send()

    for n in range(NCH):
        for flow in (S_SIB, S_PART, S_REST, S_FAR_UP, S_FAR_DOWN, S_FAR_SIB, S_FAR_REST):
            to_near(near_part(SIB, n), SIB, n, flow, (sibling, v)).wait_send()

        @pl.when(jnp.logical_not(last))
        def _():
            to_near(near_part(SIB, n), SIB, n, S_UP, (sibling, v)).wait_send()

        @pl.when(jnp.logical_not(first))
        def _():
            to_near(near_part(SIB, n), SIB, n, S_DOWN, (sibling, v)).wait_send()

        @pl.when(edge)
        def _():
            to_near(near_part(SIB, n), SIB, n, S_WRAP, (sibling, v)).wait_send()
            to_near(near_part(SIB, n), SIB, n, S_CROSS, (sibling, v)).wait_send()

    for copy in round_two:
        copy.wait()
    for k in range(3):
        total = total + next_in[k]
    summed = jnp.sum(total, axis=1, keepdims=True) / NVIR
    for k in range(3):
        trace[0:1, k:k + 1] = summed[k:k + 1, :]


def local(factor, occ_energy, vir_energy):
    vmem = pl.BlockSpec(memory_space=pltpu.VMEM)
    dma = pltpu.SemaphoreType.DMA
    block = (ROWS, NAUX)
    return pl.pallas_call(
        kernel,
        out_shape=(
            jax.ShapeDtypeStruct((1,) + block, F32),
            jax.ShapeDtypeStruct((1, 3), F32),
        ),
        in_specs=[pl.BlockSpec(memory_space=pltpu.HBM), vmem, vmem],
        out_specs=(vmem, vmem),
        scratch_shapes=[
            pltpu.VMEM(block, F32),
            pltpu.VMEM((5,) + block, F32),
            pltpu.VMEM((5,) + block, F32),
            pltpu.VMEM(block, F32),
            pltpu.VMEM((5 * ROWS, NAUX), BF16),
            pltpu.VMEM((5 * ROWS, NAUX), BF16),
            pltpu.VMEM(block, BF16),
            pltpu.VMEM(block, BF16),
            pltpu.VMEM((5, ROWS, 128), F32),
            pltpu.VMEM((8, 128), F32),
            pltpu.VMEM((5, 8, 128), F32),
            pltpu.VMEM((5, 8, 128), F32),
            pltpu.VMEM((8, 128), F32),
            pltpu.VMEM((7, 8, 128), F32),
            pltpu.VMEM((8, 128), F32),
            pltpu.VMEM((3, 8, 128), F32),
            dma,
            dma((11, NCH)),
            dma((5, NCH)),
            dma((5, NCH)),
            dma((NCH,)),
            dma((5,)),
            dma((5,)),
            dma((10,)),
            dma((10,)),
        ],
        compiler_params=pltpu.CompilerParams(
            collective_id=0, has_side_effects=True, vmem_limit_bytes=48 << 20
        ),
        cost_estimate=pl.CostEstimate(
            flops=6 * 24 * ROWS * ROWS * NAUX, bytes_accessed=2 * 4 * ROWS * NAUX, transcendentals=0
        ),
    )(factor, occ_energy.reshape(1, 1), vir_energy.reshape(1, 128))


def solution(mesh):
    placed = (P("occ", "vir", None), P("occ"), P("vir"))
    return jax.shard_map(
        local,
        mesh=mesh,
        in_specs=placed,
        out_specs=(P("occ", "vir", None), P("occ", None)),
        check_vma=False,
    )
```

```python
import jax
import jax.numpy as jnp
from jax import lax
from jax.experimental import pallas as pl
from jax.experimental.pallas import tpu as pltpu
from jax.sharding import PartitionSpec as P

NVIR = 4096
NAUX = 1280
ROWS = 128
NCH = 4
CH = ROWS // NCH
COLS = 256
MESH = pl.DeviceIdType.MESH
F32 = jnp.float32
BF16 = jnp.bfloat16

OWN, SIB, UP, DOWN, REST = range(5)
(
    S_SIB, S_UP, S_DOWN, S_PART, S_REST, S_FAR_UP, S_FAR_DOWN, S_FAR_SIB, S_FAR_REST,
    S_WRAP, S_CROSS,
) = range(11)


def halves(value):
    high = value.astype(BF16)
    return high, (value - high.astype(F32)).astype(BF16)


def rows_dot(former, latter):
    dims = (((1,), (1,)), ((), ()))

    def dot(a, b):
        return lax.dot_general(a, b, dims, preferred_element_type=F32)

    return dot(former[0], latter[0]) + (dot(former[0], latter[1]) + dot(former[1], latter[0]))


def folded(tile):
    return jnp.sum(tile.reshape(tile.shape[0] // 8, 8, 128), axis=0)


def kernel(
    factor, occ, vir, density, trace,
    own, near, far, staged, near_h, near_l, far_h, far_l, crossed, energy, energies, sums,
    other_tile, tile_out, tile_in, next_out, next_in,
    own_sem, send_sem, near_sem, far_sem, staged_sem, e_send, e_recv, t_send, t_recv,
    x_send, x_recv, entered,
):
    o = lax.axis_index("occ")
    v = lax.axis_index("vir")
    q = lax.rem(o, 2)
    x = lax.rem(o // 2, 4)
    y_lo = o // 8
    other_row = o + 8 - 16 * y_lo
    sibling = o + 1 - 2 * q
    mate = v + 1 - 2 * lax.rem(v, 2)
    first = x == 0
    last = x == 3
    edge = jnp.logical_or(first, last)
    inner = jnp.logical_not(edge)
    across = jnp.where(last, o - 6, o + 6)

    def occ_at(distance):
        return lax.rem(o + distance + 16, 16)

    up, down = occ_at(2), occ_at(-2)
    beyond = jnp.where(last, up, down)

    half = lax.rem(v, 2)

    def vir_at(distance):
        return lax.rem(v + 2 * distance + 32, 32)

    own_copy = pltpu.make_async_copy(factor.at[0], own, own_sem)
    own_copy.start()

    barrier = pltpu.get_barrier_semaphore()
    peers = [(occ_at(d), v) for d in (1, -1, 2, -2)]
    peers += [(o, mate), (o, vir_at(1)), (o, vir_at(-1))]
    for peer in peers:
        pl.semaphore_signal(barrier, inc=1, device_id=peer, device_id_type=MESH)

    @pl.when(edge)
    def _():
        for peer in ((other_row, v), (across, v), (other_row, mate), (beyond, mate)):
            pl.semaphore_signal(barrier, inc=1, device_id=peer, device_id_type=MESH)

    energy[...] = jnp.zeros((8, 128), F32)
    energy[0:1, :] = vir[...]
    energy[1:2, :] = jnp.broadcast_to(occ[...], (1, 128))

    pl.semaphore_wait(barrier, jnp.where(edge, len(peers) + 4, len(peers)))

    def remote(src, dst, send, recv, device):
        return pltpu.make_async_remote_copy(
            src_ref=src, dst_ref=dst, send_sem=send, recv_sem=recv,
            device_id=device, device_id_type=MESH,
        )

    def part(ref, n):
        return ref.at[pl.ds(n * CH, CH)]

    def mine(n):
        return factor.at[0, pl.ds(n * CH, CH)]

    def to_near(src, slot, n, flow, device):
        return remote(
            src, near.at[slot, pl.ds(n * CH, CH)], send_sem.at[flow, n], near_sem.at[slot, n], device
        )

    def to_far(src, slot, n, flow, device):
        return remote(
            src, far.at[slot, pl.ds(n * CH, CH)], send_sem.at[flow, n], far_sem.at[slot, n], device
        )

    def to_staged(n):
        return remote(
            mine(n), part(staged, n), send_sem.at[S_PART, n], staged_sem.at[n], (other_row, v)
        )

    def near_part(slot, n):
        return near.at[slot, pl.ds(n * CH, CH)]

    def far_part(slot, n):
        return far.at[slot, pl.ds(n * CH, CH)]

    e_peers = [(occ_at(1), v), (occ_at(-1), v), (occ_at(2), v), (occ_at(-2), v), (o, mate)]
    e_copies = [
        remote(energy, energies.at[k], e_send.at[k], e_recv.at[k], peer)
        for k, peer in enumerate(e_peers)
    ]
    for copy in e_copies:
        copy.start()

    def far_wrap(n):
        @pl.when(last)
        def _():
            to_far(mine(n), DOWN, n, S_FAR_UP, (up, mate)).start()

        @pl.when(first)
        def _():
            to_far(mine(n), UP, n, S_FAR_DOWN, (down, mate)).start()

    for n in range(NCH):
        @pl.when(edge)
        def _():
            to_staged(n).start()

        if n == 0:
            far_wrap(0)

        @pl.when(inner)
        def _():
            to_far(mine(n), 0, n, S_PART, (o, mate)).start()

        @pl.when(jnp.logical_not(last))
        def _():
            to_near(mine(n), DOWN, n, S_UP, (up, v)).start()

        @pl.when(jnp.logical_not(first))
        def _():
            to_near(mine(n), UP, n, S_DOWN, (down, v)).start()

        to_near(mine(n), SIB, n, S_SIB, (sibling, v)).start()

    def wait_near(slot, n):
        to_near(near_part(slot, n), slot, n, S_SIB, (sibling, v)).wait_recv()

    def wait_far(slot, n):
        to_far(far_part(slot, n), slot, n, S_SIB, (sibling, v)).wait_recv()

    def relay_staged(n):
        @pl.when(edge)
        def _():
            to_staged(n).wait_recv()
            to_near(part(staged, n), jnp.where(last, DOWN, UP), n, S_WRAP, (across, v)).start()
            to_far(part(staged, n), 0, n, S_CROSS, (other_row, mate)).start()

    def relay_partner(n):
        wait_far(0, n)

        @pl.when(jnp.logical_not(last))
        def _():
            to_far(far_part(0, n), DOWN, n, S_FAR_UP, (up, v)).start()

        @pl.when(jnp.logical_not(first))
        def _():
            to_far(far_part(0, n), UP, n, S_FAR_DOWN, (down, v)).start()

        if n + 1 < NCH:
            far_wrap(n + 1)
        to_far(far_part(0, n), SIB, n, S_FAR_SIB, (sibling, v)).start()

    passed = jnp.where(q == 0, UP, DOWN)

    def relay_near(n):
        wait_near(UP, n)
        wait_near(DOWN, n)
        to_near(near_part(passed, n), REST, n, S_REST, (sibling, v)).start()

    def relay_far(n):
        wait_far(UP, n)
        wait_far(DOWN, n)
        to_far(far_part(passed, n), REST, n, S_FAR_REST, (sibling, v)).start()

    def split_near(slot, start, count):
        rows = pl.ds(slot * ROWS + start, count)
        h, l = halves(near[slot, pl.ds(start, count), :])
        near_h[rows, :] = h
        near_l[rows, :] = l

    def split_far(slot, start, count):
        rows = pl.ds(slot * ROWS + start, count)
        h, l = halves(far[slot, pl.ds(start, count), :])
        far_h[rows, :] = h
        far_l[rows, :] = l

    def near_rows(slot, count=1):
        rows = pl.ds(slot * ROWS, count * ROWS)
        return near_h[rows, :], near_l[rows, :]

    def add_density(weights, latter_h, latter_l, fresh=False):
        w_h, w_l = halves(weights)
        for c in range(NAUX // COLS):
            cols = pl.ds(c * COLS, COLS)
            h, l = latter_h[:, cols], latter_l[:, cols]
            term = (
                jnp.dot(w_h, h, preferred_element_type=F32)
                + jnp.dot(w_h, l, preferred_element_type=F32)
                + jnp.dot(w_l, h, preferred_element_type=F32)
            )
            density[0, :, cols] = term if fresh else density[0, :, cols] + term

    def pair_energy(slot):
        if slot == OWN:
            row = energy[1:2, :]
        elif slot == UP:
            row = energies[3, 1:2, :]
        elif slot == DOWN:
            row = energies[2, 1:2, :]
        elif slot == SIB:
            row = jnp.where(q == 0, energies[1, 1:2, :], energies[0, 1:2, :])
        else:
            row = jnp.where(q == 0, energies[0, 1:2, :], energies[1, 1:2, :])
        return row + energy[1:2, :]

    def diag_weights(k_tile, slot):
        across_b = jnp.broadcast_to(energy[0:1, :], (ROWS, 128))
        gap = pair_energy(slot) - across_b.T - across_b
        amp = k_tile / gap
        bar = 2.0 * amp - amp.T
        sums[slot] = folded(amp * bar)
        return 2.0 * bar if slot == OWN else bar

    def greet(step):
        pl.semaphore_signal(
            entered.at[step, 0], inc=1, device_id=(o, vir_at(-(1 << step))), device_id_type=MESH
        )
        pl.semaphore_signal(
            entered.at[step, 1], inc=1, device_id=(o, vir_at(1 << step)), device_id_type=MESH
        )

    def greeted(step):
        pl.semaphore_wait(entered.at[step, 0], 1)
        pl.semaphore_wait(entered.at[step, 1], 1)

    greet(0)
    relay_staged(0)
    own_copy.wait()
    h, l = halves(own[...])
    near_h[0:ROWS, :] = h
    near_l[0:ROWS, :] = l
    for copy in e_copies:
        copy.wait()
    for n in range(NCH):
        wait_near(SIB, n)
    split_near(SIB, 0, ROWS)
    k_first = rows_dot(near_rows(OWN), near_rows(OWN, 2))
    bars = jnp.concatenate(
        [diag_weights(k_first[:, :128], OWN), diag_weights(k_first[:, 128:], SIB)], axis=1
    )
    add_density(bars, near_h.at[0:256], near_l.at[0:256], fresh=True)

    for n in range(1, NCH + 1):
        if n < NCH:
            relay_staged(n)
        relay_partner(n - 1)
        relay_near(n - 1)
        if n <= 3:
            greeted(n - 1)
            if n < 3:
                greet(n)
        start = (n - 1) * CH
        split_far(0, start, CH)
        split_near(UP, start, CH)
        split_near(DOWN, start, CH)

    for n in range(NCH):
        wait_near(REST, n)
    split_near(REST, 0, ROWS)

    far_row = jnp.broadcast_to(energies[4, 0:1, :], (ROWS, 128)).T
    own_row = jnp.broadcast_to(energy[0:1, :], (ROWS, 128))
    partner = (far_h[0:ROWS, :], far_l[0:ROWS, :])
    k_cross = rows_dot(partner, near_rows(OWN, 5))
    for slot in range(5):
        amp = k_cross[:, slot * 128:(slot + 1) * 128] / (pair_energy(slot) - far_row - own_row)
        crossed[slot] = amp
        squares = folded(amp * amp)
        sums[5 + slot] = squares if slot == OWN else 2.0 * squares

    swap = remote(
        crossed.at[jnp.where(half == 0, jnp.where(q == 0, SIB, REST), UP)],
        other_tile, x_send, x_recv, (jnp.where(half == 0, occ_at(1), up), v),
    )
    swap.start()

    k_next = rows_dot(near_rows(OWN), near_rows(UP, 3))
    bars = jnp.concatenate(
        [diag_weights(k_next[:, at * 128:(at + 1) * 128], slot) for at, slot in enumerate((UP, DOWN, REST))],
        axis=1,
    )
    add_density(bars, near_h.at[256:640], near_l.at[256:640])
    add_density(2.0 * crossed[OWN].T, far_h.at[0:ROWS], far_l.at[0:ROWS])

    def trace_one():
        swap.wait()
        here = crossed[jnp.where(half == 0, jnp.where(q == 0, REST, SIB), DOWN)]
        product = 2.0 * folded(here * other_tile[...])
        before = jnp.where(q == 0, sums[REST] + sums[5 + REST], sums[SIB] + sums[5 + SIB])
        before = before - jnp.where(half == 0, product, 0.0)
        second = sums[DOWN] + sums[5 + DOWN] - jnp.where(half == 0, 0.0, product)
        tile_out[...] = jnp.zeros((8, 128), F32)
        tile_out[0:1, :] = jnp.sum(sums[OWN] + sums[5 + OWN], axis=0, keepdims=True)
        tile_out[1:2, :] = jnp.sum(before, axis=0, keepdims=True)
        tile_out[2:3, :] = jnp.sum(second, axis=0, keepdims=True)
        for copy in round_one:
            copy.start()

    def trace_two():
        total = tile_out[...]
        for copy in round_one:
            copy.wait_recv()
        for r in range(7):
            total = total + tile_in[r]
        next_out[...] = total
        for copy in round_two:
            copy.start()

    near_z = [(0, mate)] + [(d, side) for d in (1, 2, 3) for side in (v, mate)]
    round_one = [
        remote(
            tile_out, tile_in.at[k], t_send.at[k], t_recv.at[k],
            (o, lax.rem(side + 2 * d, 32)),
        )
        for k, (d, side) in enumerate(near_z)
    ]
    round_two = [
        remote(next_out, next_in.at[k], t_send.at[7 + k], t_recv.at[7 + k], (o, vir_at(d)))
        for k, d in enumerate((4, 8, -4))
    ]

    own_pair = near_rows(OWN)
    for n in range(NCH):
        relay_far(n)
        start = n * CH
        wait_far(SIB, n)
        wait_far(REST, n)
        for at, slot in enumerate((SIB, UP, DOWN, REST)):
            h, l = halves(far[slot, pl.ds(start, CH), :])
            far_h[at * CH:(at + 1) * CH, :] = h
            far_l[at * CH:(at + 1) * CH, :] = l
        k_tile = rows_dot((far_h[...], far_l[...]), own_pair)
        bars = []
        side = far_row[start:start + CH, :]
        for at, slot in enumerate((SIB, UP, DOWN, REST)):
            gap = pair_energy(slot) - side - own_row[0:CH, :]
            amp = k_tile[at * CH:(at + 1) * CH, :] / gap
            bars.append(2.0 * amp - crossed[slot, pl.ds(start, CH), :])
        add_density(jnp.concatenate(bars, axis=0).T, far_h, far_l)
        if n == 0:
            trace_one()
        elif n == NCH - 2:
            trace_two()

    for copy in round_one:
        copy.wait_send()

    for n in range(NCH):
        for flow in (S_SIB, S_PART, S_REST, S_FAR_UP, S_FAR_DOWN, S_FAR_SIB, S_FAR_REST):
            to_near(near_part(SIB, n), SIB, n, flow, (sibling, v)).wait_send()

        @pl.when(jnp.logical_not(last))
        def _():
            to_near(near_part(SIB, n), SIB, n, S_UP, (sibling, v)).wait_send()

        @pl.when(jnp.logical_not(first))
        def _():
            to_near(near_part(SIB, n), SIB, n, S_DOWN, (sibling, v)).wait_send()

        @pl.when(edge)
        def _():
            to_near(near_part(SIB, n), SIB, n, S_WRAP, (sibling, v)).wait_send()
            to_near(near_part(SIB, n), SIB, n, S_CROSS, (sibling, v)).wait_send()

    for copy in round_two:
        copy.wait()
    total = next_out[...]
    for k in range(3):
        total = total + next_in[k]
    summed = jnp.sum(total, axis=1, keepdims=True) / NVIR
    for k in range(3):
        trace[0:1, k:k + 1] = summed[k:k + 1, :]


def local(factor, occ_energy, vir_energy):
    vmem = pl.BlockSpec(memory_space=pltpu.VMEM)
    dma = pltpu.SemaphoreType.DMA
    block = (ROWS, NAUX)
    return pl.pallas_call(
        kernel,
        out_shape=(
            jax.ShapeDtypeStruct((1,) + block, F32),
            jax.ShapeDtypeStruct((1, 3), F32),
        ),
        in_specs=[pl.BlockSpec(memory_space=pltpu.HBM), vmem, vmem],
        out_specs=(vmem, vmem),
        scratch_shapes=[
            pltpu.VMEM(block, F32),
            pltpu.VMEM((5,) + block, F32),
            pltpu.VMEM((5,) + block, F32),
            pltpu.VMEM(block, F32),
            pltpu.VMEM((5 * ROWS, NAUX), BF16),
            pltpu.VMEM((5 * ROWS, NAUX), BF16),
            pltpu.VMEM(block, BF16),
            pltpu.VMEM(block, BF16),
            pltpu.VMEM((5, ROWS, 128), F32),
            pltpu.VMEM((8, 128), F32),
            pltpu.VMEM((5, 8, 128), F32),
            pltpu.VMEM((10, 8, 128), F32),
            pltpu.VMEM((ROWS, 128), F32),
            pltpu.VMEM((8, 128), F32),
            pltpu.VMEM((7, 8, 128), F32),
            pltpu.VMEM((8, 128), F32),
            pltpu.VMEM((3, 8, 128), F32),
            dma,
            dma((11, NCH)),
            dma((5, NCH)),
            dma((5, NCH)),
            dma((NCH,)),
            dma((5,)),
            dma((5,)),
            dma((10,)),
            dma((10,)),
            dma,
            dma,
            pltpu.SemaphoreType.REGULAR((3, 2)),
        ],
        compiler_params=pltpu.CompilerParams(
            collective_id=0, has_side_effects=True, vmem_limit_bytes=62 << 20
        ),
        cost_estimate=pl.CostEstimate(
            flops=6 * 24 * ROWS * ROWS * NAUX, bytes_accessed=2 * 4 * ROWS * NAUX, transcendentals=0
        ),
    )(factor, occ_energy.reshape(1, 1), vir_energy.reshape(1, 128))


def solution(mesh):
    placed = (P("occ", "vir", None), P("occ"), P("vir"))
    return jax.shard_map(
        local,
        mesh=mesh,
        in_specs=placed,
        out_specs=(P("occ", "vir", None), P("occ", None)),
        check_vma=False,
    )
```

```python
import jax
import jax.numpy as jnp
from jax import lax
from jax.experimental import pallas as pl
from jax.experimental.pallas import tpu as pltpu
from jax.sharding import PartitionSpec as P

NVIR = 4096
NAUX = 1280
ROWS = 128
NCH = 4
CH = ROWS // NCH
COLS = 256
MESH = pl.DeviceIdType.MESH
F32 = jnp.float32
BF16 = jnp.bfloat16

OWN, SIB, UP, DOWN, REST = range(5)
(
    S_SIB, S_UP, S_DOWN, S_PART, S_REST, S_FAR_UP, S_FAR_DOWN, S_FAR_SIB, S_FAR_REST,
    S_WRAP, S_CROSS,
) = range(11)


def halves(value):
    high = value.astype(BF16)
    return high, (value - high.astype(F32)).astype(BF16)


def rows_dot(former, latter):
    dims = (((1,), (1,)), ((), ()))

    def dot(a, b):
        return lax.dot_general(a, b, dims, preferred_element_type=F32)

    return dot(former[0], latter[0]) + (dot(former[0], latter[1]) + dot(former[1], latter[0]))


def folded(tile):
    return jnp.sum(tile.reshape(tile.shape[0] // 8, 8, 128), axis=0)


def kernel(
    factor, occ, vir, density, trace,
    own, near, far, staged, near_h, near_l, far_h, far_l, crossed, energy, energies, sums,
    other_tile, tile_out, tile_in, next_out, next_in,
    own_sem, send_sem, near_sem, far_sem, staged_sem, e_send, e_recv, t_send, t_recv,
    x_send, x_recv, entered,
):
    o = lax.axis_index("occ")
    v = lax.axis_index("vir")
    q = lax.rem(o, 2)
    x = lax.rem(o // 2, 4)
    y_lo = o // 8
    other_row = o + 8 - 16 * y_lo
    sibling = o + 1 - 2 * q
    mate = v + 1 - 2 * lax.rem(v, 2)
    first = x == 0
    last = x == 3
    edge = jnp.logical_or(first, last)
    inner = jnp.logical_not(edge)
    across = jnp.where(last, o - 6, o + 6)

    def occ_at(distance):
        return lax.rem(o + distance + 16, 16)

    up, down = occ_at(2), occ_at(-2)
    beyond = jnp.where(last, up, down)

    half = lax.rem(v, 2)
    z = v // 2
    below, above = z > 0, z < 15

    def flipped(r):
        out = v
        for bit in (1, 2, 4, 8, 16):
            if r & bit:
                out = out + bit - 2 * bit * lax.rem(v // bit, 2)
        return out

    own_copy = pltpu.make_async_copy(factor.at[0], own, own_sem)
    own_copy.start()

    barrier = pltpu.get_barrier_semaphore()
    peers = [(occ_at(d), v) for d in (1, -1, 2, -2)]
    peers += [(o, mate)]
    for peer in peers:
        pl.semaphore_signal(barrier, inc=1, device_id=peer, device_id_type=MESH)

    @pl.when(edge)
    def _():
        for peer in ((other_row, v), (across, v), (other_row, mate), (beyond, mate)):
            pl.semaphore_signal(barrier, inc=1, device_id=peer, device_id_type=MESH)

    @pl.when(below)
    def _():
        pl.semaphore_signal(barrier, inc=1, device_id=(o, v - 2), device_id_type=MESH)

    @pl.when(above)
    def _():
        pl.semaphore_signal(barrier, inc=1, device_id=(o, v + 2), device_id_type=MESH)

    energy[...] = jnp.zeros((8, 128), F32)
    energy[0:1, :] = vir[...]
    energy[1:2, :] = jnp.broadcast_to(occ[...], (1, 128))

    at_end = jnp.where(jnp.logical_and(below, above), 0, 1)
    pl.semaphore_wait(barrier, jnp.where(edge, len(peers) + 6, len(peers) + 2) - at_end)

    def remote(src, dst, send, recv, device):
        return pltpu.make_async_remote_copy(
            src_ref=src, dst_ref=dst, send_sem=send, recv_sem=recv,
            device_id=device, device_id_type=MESH,
        )

    def part(ref, n):
        return ref.at[pl.ds(n * CH, CH)]

    def mine(n):
        return factor.at[0, pl.ds(n * CH, CH)]

    def to_near(src, slot, n, flow, device):
        return remote(
            src, near.at[slot, pl.ds(n * CH, CH)], send_sem.at[flow, n], near_sem.at[slot, n], device
        )

    def to_far(src, slot, n, flow, device):
        return remote(
            src, far.at[slot, pl.ds(n * CH, CH)], send_sem.at[flow, n], far_sem.at[slot, n], device
        )

    def to_staged(n):
        return remote(
            mine(n), part(staged, n), send_sem.at[S_PART, n], staged_sem.at[n], (other_row, v)
        )

    def near_part(slot, n):
        return near.at[slot, pl.ds(n * CH, CH)]

    def far_part(slot, n):
        return far.at[slot, pl.ds(n * CH, CH)]

    e_peers = [(occ_at(1), v), (occ_at(-1), v), (occ_at(2), v), (occ_at(-2), v), (o, mate)]
    e_copies = [
        remote(energy, energies.at[k], e_send.at[k], e_recv.at[k], peer)
        for k, peer in enumerate(e_peers)
    ]
    for copy in e_copies:
        copy.start()

    def far_wrap(n):
        @pl.when(last)
        def _():
            to_far(mine(n), DOWN, n, S_FAR_UP, (up, mate)).start()

        @pl.when(first)
        def _():
            to_far(mine(n), UP, n, S_FAR_DOWN, (down, mate)).start()

    for n in range(NCH):
        @pl.when(edge)
        def _():
            to_staged(n).start()

        if n == 0:
            far_wrap(0)

        @pl.when(inner)
        def _():
            to_far(mine(n), 0, n, S_PART, (o, mate)).start()

        @pl.when(jnp.logical_not(last))
        def _():
            to_near(mine(n), DOWN, n, S_UP, (up, v)).start()

        @pl.when(jnp.logical_not(first))
        def _():
            to_near(mine(n), UP, n, S_DOWN, (down, v)).start()

        to_near(mine(n), SIB, n, S_SIB, (sibling, v)).start()

    def wait_near(slot, n):
        to_near(near_part(slot, n), slot, n, S_SIB, (sibling, v)).wait_recv()

    def wait_far(slot, n):
        to_far(far_part(slot, n), slot, n, S_SIB, (sibling, v)).wait_recv()

    def relay_staged(n):
        @pl.when(edge)
        def _():
            to_staged(n).wait_recv()
            to_near(part(staged, n), jnp.where(last, DOWN, UP), n, S_WRAP, (across, v)).start()
            to_far(part(staged, n), 0, n, S_CROSS, (other_row, mate)).start()

    def take_partner(n):
        wait_far(0, n)
        to_far(far_part(0, n), SIB, n, S_FAR_SIB, (sibling, v)).start()

    def relay_partner(n):
        @pl.when(jnp.logical_not(last))
        def _():
            to_far(far_part(0, n), DOWN, n, S_FAR_UP, (up, v)).start()

        @pl.when(jnp.logical_not(first))
        def _():
            to_far(far_part(0, n), UP, n, S_FAR_DOWN, (down, v)).start()

    passed = jnp.where(q == 0, UP, DOWN)

    def relay_near(n):
        wait_near(UP, n)
        wait_near(DOWN, n)
        to_near(near_part(passed, n), REST, n, S_REST, (sibling, v)).start()

    def relay_far(n):
        wait_far(UP, n)
        wait_far(DOWN, n)
        to_far(far_part(passed, n), REST, n, S_FAR_REST, (sibling, v)).start()

    def split_near(slot, start, count):
        rows = pl.ds(slot * ROWS + start, count)
        h, l = halves(near[slot, pl.ds(start, count), :])
        near_h[rows, :] = h
        near_l[rows, :] = l

    def split_far(slot, start, count):
        rows = pl.ds(slot * ROWS + start, count)
        h, l = halves(far[slot, pl.ds(start, count), :])
        far_h[rows, :] = h
        far_l[rows, :] = l

    def near_rows(slot, count=1):
        rows = pl.ds(slot * ROWS, count * ROWS)
        return near_h[rows, :], near_l[rows, :]

    def add_density(weights, latter_h, latter_l, fresh=False):
        w_h, w_l = halves(weights)
        for c in range(NAUX // COLS):
            cols = pl.ds(c * COLS, COLS)
            h, l = latter_h[:, cols], latter_l[:, cols]
            term = (
                jnp.dot(w_h, h, preferred_element_type=F32)
                + jnp.dot(w_h, l, preferred_element_type=F32)
                + jnp.dot(w_l, h, preferred_element_type=F32)
            )
            density[0, :, cols] = term if fresh else density[0, :, cols] + term

    def pair_energy(slot):
        if slot == OWN:
            row = energy[1:2, :]
        elif slot == UP:
            row = energies[3, 1:2, :]
        elif slot == DOWN:
            row = energies[2, 1:2, :]
        elif slot == SIB:
            row = jnp.where(q == 0, energies[1, 1:2, :], energies[0, 1:2, :])
        else:
            row = jnp.where(q == 0, energies[0, 1:2, :], energies[1, 1:2, :])
        return row + energy[1:2, :]

    def diag_weights(k_tile, slot):
        across_b = jnp.broadcast_to(energy[0:1, :], (ROWS, 128))
        gap = pair_energy(slot) - across_b.T - across_b
        amp = k_tile / gap
        bar = 2.0 * amp - amp.T
        sums[slot] = folded(amp * bar)
        return 2.0 * bar if slot == OWN else bar

    def greet(step):
        @pl.when(z >= 1 << step)
        def _():
            pl.semaphore_signal(
                entered.at[step, 0], inc=1, device_id=(o, v - (2 << step)), device_id_type=MESH
            )

        @pl.when(z < 16 - (1 << step))
        def _():
            pl.semaphore_signal(
                entered.at[step, 1], inc=1, device_id=(o, v + (2 << step)), device_id_type=MESH
            )

    def greeted(step):
        @pl.when(z < 16 - (1 << step))
        def _():
            pl.semaphore_wait(entered.at[step, 0], 1)

        @pl.when(z >= 1 << step)
        def _():
            pl.semaphore_wait(entered.at[step, 1], 1)

    greet(0)
    relay_staged(0)
    own_copy.wait()
    h, l = halves(own[...])
    near_h[0:ROWS, :] = h
    near_l[0:ROWS, :] = l
    for copy in e_copies:
        copy.wait()
    for n in range(NCH):
        wait_near(SIB, n)
    split_near(SIB, 0, ROWS)
    k_first = rows_dot(near_rows(OWN), near_rows(OWN, 2))
    bars = jnp.concatenate(
        [diag_weights(k_first[:, :128], OWN), diag_weights(k_first[:, 128:], SIB)], axis=1
    )
    add_density(bars, near_h.at[0:256], near_l.at[0:256], fresh=True)

    for n in range(1, NCH + 1):
        if n < NCH:
            relay_staged(n)
        take_partner(n - 1)
        relay_near(n - 1)
        relay_partner(n - 1)
        if n == NCH:
            for m in range(1, NCH):
                far_wrap(m)
        if n == 1:
            greeted(0)
            greet(1)
        elif n == 2:
            greeted(1)
            greet(2)
        elif n == NCH:
            greeted(2)
            greet(3)
        start = (n - 1) * CH
        split_far(0, start, CH)
        split_near(UP, start, CH)
        split_near(DOWN, start, CH)

    for n in range(NCH):
        wait_near(REST, n)
    split_near(REST, 0, ROWS)

    far_row = jnp.broadcast_to(energies[4, 0:1, :], (ROWS, 128)).T
    own_row = jnp.broadcast_to(energy[0:1, :], (ROWS, 128))
    partner = (far_h[0:ROWS, :], far_l[0:ROWS, :])
    k_cross = rows_dot(partner, near_rows(OWN, 5))
    for slot in range(5):
        amp = k_cross[:, slot * 128:(slot + 1) * 128] / (pair_energy(slot) - far_row - own_row)
        crossed[slot] = amp
        squares = folded(amp * amp)
        sums[5 + slot] = squares if slot == OWN else 2.0 * squares

    before = jnp.where(q == 0, REST, SIB)
    swap = remote(
        crossed.at[jnp.where(half == 0, DOWN, before)], other_tile, x_send, x_recv, (o, mate)
    )
    swap.start()

    k_next = rows_dot(near_rows(OWN), near_rows(UP, 3))
    bars = jnp.concatenate(
        [diag_weights(k_next[:, at * 128:(at + 1) * 128], slot) for at, slot in enumerate((UP, DOWN, REST))],
        axis=1,
    )
    def trace_one():
        swap.wait()
        here = crossed[jnp.where(half == 0, before, DOWN)]
        product = 2.0 * folded(here * other_tile[...].T)
        first = jnp.where(q == 0, sums[REST] + sums[5 + REST], sums[SIB] + sums[5 + SIB])
        first = first - jnp.where(half == 0, product, 0.0)
        second = sums[DOWN] + sums[5 + DOWN] - jnp.where(half == 0, 0.0, product)
        tile_out[...] = jnp.zeros((8, 128), F32)
        tile_out[0:1, :] = jnp.sum(sums[OWN] + sums[5 + OWN], axis=0, keepdims=True)
        tile_out[1:2, :] = jnp.sum(first, axis=0, keepdims=True)
        tile_out[2:3, :] = jnp.sum(second, axis=0, keepdims=True)
        for copy in round_one:
            copy.start()

    def trace_two():
        total = tile_out[...]
        for copy in round_one:
            copy.wait_recv()
        for r in range(7):
            total = total + tile_in[r]
        next_out[...] = total
        greeted(3)
        for copy in round_two:
            copy.start()

    round_one = [
        remote(tile_out, tile_in.at[r - 1], t_send.at[r - 1], t_recv.at[r - 1], (o, flipped(r)))
        for r in range(1, 8)
    ]
    round_two = [
        remote(next_out, next_in.at[k], t_send.at[7 + k], t_recv.at[7 + k], (o, flipped(r)))
        for k, r in enumerate((8, 16, 24))
    ]

    trace_one()
    add_density(bars, near_h.at[256:640], near_l.at[256:640])
    add_density(2.0 * crossed[OWN].T, far_h.at[0:ROWS], far_l.at[0:ROWS])

    own_pair = near_rows(OWN)
    for n in range(NCH):
        relay_far(n)
        start = n * CH
        wait_far(SIB, n)
        wait_far(REST, n)
        for at, slot in enumerate((SIB, UP, DOWN, REST)):
            h, l = halves(far[slot, pl.ds(start, CH), :])
            far_h[at * CH:(at + 1) * CH, :] = h
            far_l[at * CH:(at + 1) * CH, :] = l
        k_tile = rows_dot((far_h[...], far_l[...]), own_pair)
        bars = []
        side = far_row[start:start + CH, :]
        for at, slot in enumerate((SIB, UP, DOWN, REST)):
            gap = pair_energy(slot) - side - own_row[0:CH, :]
            amp = k_tile[at * CH:(at + 1) * CH, :] / gap
            bars.append(2.0 * amp - crossed[slot, pl.ds(start, CH), :])
        add_density(jnp.concatenate(bars, axis=0).T, far_h, far_l)
        if n == 0:
            trace_two()

    for copy in round_one:
        copy.wait_send()

    for n in range(NCH):
        for flow in (S_SIB, S_PART, S_REST, S_FAR_UP, S_FAR_DOWN, S_FAR_SIB, S_FAR_REST):
            to_near(near_part(SIB, n), SIB, n, flow, (sibling, v)).wait_send()

        @pl.when(jnp.logical_not(last))
        def _():
            to_near(near_part(SIB, n), SIB, n, S_UP, (sibling, v)).wait_send()

        @pl.when(jnp.logical_not(first))
        def _():
            to_near(near_part(SIB, n), SIB, n, S_DOWN, (sibling, v)).wait_send()

        @pl.when(edge)
        def _():
            to_near(near_part(SIB, n), SIB, n, S_WRAP, (sibling, v)).wait_send()
            to_near(near_part(SIB, n), SIB, n, S_CROSS, (sibling, v)).wait_send()

    for copy in round_two:
        copy.wait()
    total = next_out[...]
    for k in range(3):
        total = total + next_in[k]
    summed = jnp.sum(total, axis=1, keepdims=True) / NVIR
    for k in range(3):
        trace[0:1, k:k + 1] = summed[k:k + 1, :]


def local(factor, occ_energy, vir_energy):
    vmem = pl.BlockSpec(memory_space=pltpu.VMEM)
    dma = pltpu.SemaphoreType.DMA
    block = (ROWS, NAUX)
    return pl.pallas_call(
        kernel,
        out_shape=(
            pltpu.VMEM((1,) + block, F32),
            jax.ShapeDtypeStruct((1, 3), F32),
        ),
        in_specs=[pl.BlockSpec(memory_space=pltpu.HBM), vmem, vmem],
        out_specs=(vmem, vmem),
        scratch_shapes=[
            pltpu.VMEM(block, F32),
            pltpu.VMEM((5,) + block, F32),
            pltpu.VMEM((5,) + block, F32),
            pltpu.VMEM(block, F32),
            pltpu.VMEM((5 * ROWS, NAUX), BF16),
            pltpu.VMEM((5 * ROWS, NAUX), BF16),
            pltpu.VMEM(block, BF16),
            pltpu.VMEM(block, BF16),
            pltpu.VMEM((5, ROWS, 128), F32),
            pltpu.VMEM((8, 128), F32),
            pltpu.VMEM((5, 8, 128), F32),
            pltpu.VMEM((10, 8, 128), F32),
            pltpu.VMEM((ROWS, 128), F32),
            pltpu.VMEM((8, 128), F32),
            pltpu.VMEM((7, 8, 128), F32),
            pltpu.VMEM((8, 128), F32),
            pltpu.VMEM((3, 8, 128), F32),
            dma,
            dma((11, NCH)),
            dma((5, NCH)),
            dma((5, NCH)),
            dma((NCH,)),
            dma((5,)),
            dma((5,)),
            dma((10,)),
            dma((10,)),
            dma,
            dma,
            pltpu.SemaphoreType.REGULAR((4, 2)),
        ],
        compiler_params=pltpu.CompilerParams(
            collective_id=0, has_side_effects=True, vmem_limit_bytes=62 << 20
        ),
        cost_estimate=pl.CostEstimate(
            flops=6 * 24 * ROWS * ROWS * NAUX, bytes_accessed=2 * 4 * ROWS * NAUX, transcendentals=0
        ),
    )(factor, occ_energy.reshape(1, 1), vir_energy.reshape(1, 128))


def solution(mesh):
    placed = (P("occ", "vir", None), P("occ"), P("vir"))
    return jax.shard_map(
        local,
        mesh=mesh,
        in_specs=placed,
        out_specs=(P("occ", "vir", None), P("occ", None)),
        check_vma=False,
    )
```

```python
import jax
import jax.numpy as jnp
from jax import lax
from jax.experimental import pallas as pl
from jax.experimental.pallas import tpu as pltpu
from jax.sharding import PartitionSpec as P

NVIR = 4096
NAUX = 1280
ROWS = 128
NCH = 4
CH = ROWS // NCH
COLS = 256
MESH = pl.DeviceIdType.MESH
F32 = jnp.float32
BF16 = jnp.bfloat16

OWN, SIB, UP, DOWN, REST = range(5)
(
    S_SIB, S_UP, S_DOWN, S_PART, S_REST, S_FAR_UP, S_FAR_DOWN, S_FAR_SIB, S_FAR_REST,
    S_WRAP, S_CROSS,
) = range(11)


def halves(value):
    high = value.astype(BF16)
    return high, (value - high.astype(F32)).astype(BF16)


def rows_dot(former, latter):
    dims = (((1,), (1,)), ((), ()))

    def dot(a, b):
        return lax.dot_general(a, b, dims, preferred_element_type=F32)

    return dot(former[0], latter[0]) + (dot(former[0], latter[1]) + dot(former[1], latter[0]))


def folded(tile):
    return jnp.sum(tile.reshape(tile.shape[0] // 8, 8, 128), axis=0)


def kernel(
    factor, occ, vir, density, trace,
    own, near, far, staged, near_h, near_l, far_h, far_l, crossed, energy, energies, sums,
    turned, other_tile, one_out, tile_in, next_out, next_in,
    own_sem, send_sem, near_sem, far_sem, staged_sem, e_send, e_recv, t_send, t_recv,
    x_send, x_recv, entered,
):
    o = lax.axis_index("occ")
    v = lax.axis_index("vir")
    q = lax.rem(o, 2)
    x = lax.rem(o // 2, 4)
    y_lo = o // 8
    other_row = o + 8 - 16 * y_lo
    sibling = o + 1 - 2 * q
    mate = v + 1 - 2 * lax.rem(v, 2)
    first = x == 0
    last = x == 3
    edge = jnp.logical_or(first, last)
    inner = jnp.logical_not(edge)
    across = jnp.where(last, o - 6, o + 6)

    def occ_at(distance):
        return lax.rem(o + distance + 16, 16)

    up, down = occ_at(2), occ_at(-2)
    beyond = jnp.where(last, up, down)

    half = lax.rem(v, 2)
    z = v // 2
    below, above = z > 0, z < 15

    def flipped(r):
        out = v
        for bit in (1, 2, 4, 8, 16):
            if r & bit:
                out = out + bit - 2 * bit * lax.rem(v // bit, 2)
        return out

    own_copy = pltpu.make_async_copy(factor.at[0], own, own_sem)
    own_copy.start()

    barrier = pltpu.get_barrier_semaphore()
    peers = [(occ_at(d), v) for d in (1, -1, 2, -2)]
    peers += [(o, mate)]
    for peer in peers:
        pl.semaphore_signal(barrier, inc=1, device_id=peer, device_id_type=MESH)

    @pl.when(edge)
    def _():
        for peer in ((other_row, v), (across, v), (other_row, mate), (beyond, mate)):
            pl.semaphore_signal(barrier, inc=1, device_id=peer, device_id_type=MESH)

    @pl.when(below)
    def _():
        pl.semaphore_signal(barrier, inc=1, device_id=(o, v - 2), device_id_type=MESH)

    @pl.when(above)
    def _():
        pl.semaphore_signal(barrier, inc=1, device_id=(o, v + 2), device_id_type=MESH)

    energy[...] = jnp.zeros((8, 128), F32)
    energy[0:1, :] = vir[...]
    energy[1:2, :] = jnp.broadcast_to(occ[...], (1, 128))

    at_end = jnp.where(jnp.logical_and(below, above), 0, 1)
    pl.semaphore_wait(barrier, jnp.where(edge, len(peers) + 6, len(peers) + 2) - at_end)

    def remote(src, dst, send, recv, device):
        return pltpu.make_async_remote_copy(
            src_ref=src, dst_ref=dst, send_sem=send, recv_sem=recv,
            device_id=device, device_id_type=MESH,
        )

    def part(ref, n):
        return ref.at[pl.ds(n * CH, CH)]

    def mine(n):
        return own.at[pl.ds(n * CH, CH)]

    def to_near(src, slot, n, flow, device):
        return remote(
            src, near.at[slot, pl.ds(n * CH, CH)], send_sem.at[flow, n], near_sem.at[slot, n], device
        )

    def to_far(src, slot, n, flow, device):
        return remote(
            src, far.at[slot, pl.ds(n * CH, CH)], send_sem.at[flow, n], far_sem.at[slot, n], device
        )

    def to_staged(n):
        return remote(
            mine(n), part(staged, n), send_sem.at[S_PART, n], staged_sem.at[n], (other_row, v)
        )

    def near_part(slot, n):
        return near.at[slot, pl.ds(n * CH, CH)]

    def far_part(slot, n):
        return far.at[slot, pl.ds(n * CH, CH)]

    e_peers = [(occ_at(1), v), (occ_at(-1), v), (occ_at(2), v), (occ_at(-2), v), (o, mate)]
    e_copies = [
        remote(energy, energies.at[k], e_send.at[k], e_recv.at[k], peer)
        for k, peer in enumerate(e_peers)
    ]
    for copy in e_copies:
        copy.start()

    def far_wrap(n):
        @pl.when(last)
        def _():
            to_far(mine(n), DOWN, n, S_FAR_UP, (up, mate)).start()

        @pl.when(first)
        def _():
            to_far(mine(n), UP, n, S_FAR_DOWN, (down, mate)).start()

    own_copy.wait()
    for n in range(NCH):
        @pl.when(edge)
        def _():
            to_staged(n).start()

        if n == 0:
            far_wrap(0)

        @pl.when(inner)
        def _():
            to_far(mine(n), 0, n, S_PART, (o, mate)).start()

        @pl.when(jnp.logical_not(last))
        def _():
            to_near(mine(n), DOWN, n, S_UP, (up, v)).start()

        @pl.when(jnp.logical_not(first))
        def _():
            to_near(mine(n), UP, n, S_DOWN, (down, v)).start()

        to_near(mine(n), SIB, n, S_SIB, (sibling, v)).start()

    def wait_near(slot, n):
        to_near(near_part(slot, n), slot, n, S_SIB, (sibling, v)).wait_recv()

    def wait_far(slot, n):
        to_far(far_part(slot, n), slot, n, S_SIB, (sibling, v)).wait_recv()

    def relay_staged(n):
        @pl.when(edge)
        def _():
            to_staged(n).wait_recv()
            to_near(part(staged, n), jnp.where(last, DOWN, UP), n, S_WRAP, (across, v)).start()
            to_far(part(staged, n), 0, n, S_CROSS, (other_row, mate)).start()

    def take_partner(n):
        wait_far(0, n)
        to_far(far_part(0, n), SIB, n, S_FAR_SIB, (sibling, v)).start()

    def relay_partner(n):
        @pl.when(jnp.logical_not(last))
        def _():
            to_far(far_part(0, n), DOWN, n, S_FAR_UP, (up, v)).start()

        @pl.when(jnp.logical_not(first))
        def _():
            to_far(far_part(0, n), UP, n, S_FAR_DOWN, (down, v)).start()

    passed = jnp.where(q == 0, UP, DOWN)

    def relay_near(n):
        wait_near(UP, n)
        wait_near(DOWN, n)
        to_near(near_part(passed, n), REST, n, S_REST, (sibling, v)).start()

    def relay_far(n):
        wait_far(UP, n)
        wait_far(DOWN, n)
        to_far(far_part(passed, n), REST, n, S_FAR_REST, (sibling, v)).start()

    def split_near(slot, start, count):
        rows = pl.ds(slot * ROWS + start, count)
        h, l = halves(near[slot, pl.ds(start, count), :])
        near_h[rows, :] = h
        near_l[rows, :] = l

    def split_far(slot, start, count):
        rows = pl.ds(slot * ROWS + start, count)
        h, l = halves(far[slot, pl.ds(start, count), :])
        far_h[rows, :] = h
        far_l[rows, :] = l

    def near_rows(slot, count=1):
        rows = pl.ds(slot * ROWS, count * ROWS)
        return near_h[rows, :], near_l[rows, :]

    def add_density(weights, latter_h, latter_l, fresh=False):
        w_h, w_l = halves(weights)
        for c in range(NAUX // COLS):
            cols = pl.ds(c * COLS, COLS)
            h, l = latter_h[:, cols], latter_l[:, cols]
            term = (
                jnp.dot(w_h, h, preferred_element_type=F32)
                + jnp.dot(w_h, l, preferred_element_type=F32)
                + jnp.dot(w_l, h, preferred_element_type=F32)
            )
            density[0, :, cols] = term if fresh else density[0, :, cols] + term

    def pair_energy(slot):
        if slot == OWN:
            row = energy[1:2, :]
        elif slot == UP:
            row = energies[3, 1:2, :]
        elif slot == DOWN:
            row = energies[2, 1:2, :]
        elif slot == SIB:
            row = jnp.where(q == 0, energies[1, 1:2, :], energies[0, 1:2, :])
        else:
            row = jnp.where(q == 0, energies[0, 1:2, :], energies[1, 1:2, :])
        return row + energy[1:2, :]

    def diag_weights(k_tile, slot, turned=False):
        across_b = jnp.broadcast_to(energy[0:1, :], (ROWS, 128))
        gap = pair_energy(slot) - across_b.T - across_b
        amp = k_tile / gap
        bar = 2.0 * amp.T - amp if turned else 2.0 * amp - amp.T
        sums[slot] = folded((amp.T if turned else amp) * bar)
        return 2.0 * bar if slot == OWN else bar

    def greet(step):
        @pl.when(z >= 1 << step)
        def _():
            pl.semaphore_signal(
                entered.at[step, 0], inc=1, device_id=(o, v - (2 << step)), device_id_type=MESH
            )

        @pl.when(z < 16 - (1 << step))
        def _():
            pl.semaphore_signal(
                entered.at[step, 1], inc=1, device_id=(o, v + (2 << step)), device_id_type=MESH
            )

    def greeted(step):
        @pl.when(z < 16 - (1 << step))
        def _():
            pl.semaphore_wait(entered.at[step, 0], 1)

        @pl.when(z >= 1 << step)
        def _():
            pl.semaphore_wait(entered.at[step, 1], 1)

    greet(0)
    relay_staged(0)
    h, l = halves(own[...])
    near_h[0:ROWS, :] = h
    near_l[0:ROWS, :] = l
    for copy in e_copies:
        copy.wait()
    for n in range(NCH):
        wait_near(SIB, n)
    split_near(SIB, 0, ROWS)
    k_first = rows_dot(near_rows(OWN), near_rows(OWN, 2))
    bars = jnp.concatenate(
        [diag_weights(k_first[:, :128], OWN), diag_weights(k_first[:, 128:], SIB)], axis=1
    )
    add_density(bars, near_h.at[0:256], near_l.at[0:256], fresh=True)

    far_row = jnp.broadcast_to(energies[4, 0:1, :], (ROWS, 128)).T
    own_row = jnp.broadcast_to(energy[0:1, :], (ROWS, 128))
    for n in range(1, NCH + 1):
        if n < NCH:
            relay_staged(n)
        take_partner(n - 1)
        relay_near(n - 1)
        relay_partner(n - 1)
        if n == 1:
            greeted(0)
            greet(1)
        elif n == 2:
            greeted(1)
            greet(2)
        elif n == 3:
            greeted(2)
            greet(3)
        start = (n - 1) * CH
        split_far(0, start, CH)
        split_near(UP, start, CH)
        split_near(DOWN, start, CH)
        lot = [
            jnp.concatenate(
                [near[UP * ROWS + start:UP * ROWS + start + CH, :],
                 near[DOWN * ROWS + start:DOWN * ROWS + start + CH, :],
                 far[start:start + CH, :]],
                axis=0,
            )
            for near, far in ((near_h, far_h), (near_l, far_l))
        ]
        k_lot = rows_dot(lot, near_rows(OWN, 2))
        turned[0, start:start + CH, :] = k_lot[0:CH, :128]
        turned[1, start:start + CH, :] = k_lot[CH:2 * CH, :128]
        for slot in (OWN, SIB):
            gap = pair_energy(slot) - far_row[start:start + CH, :] - own_row[0:CH, :]
            crossed[slot, start:start + CH, :] = k_lot[2 * CH:, slot * 128:(slot + 1) * 128] / gap

    for n in range(NCH):
        wait_near(REST, n)
    split_near(REST, 0, ROWS)

    k_cross = rows_dot((far_h[0:ROWS, :], far_l[0:ROWS, :]), near_rows(UP, 3))
    for at, slot in enumerate((UP, DOWN, REST)):
        crossed[slot] = k_cross[:, at * 128:(at + 1) * 128] / (pair_energy(slot) - far_row - own_row)

    before = jnp.where(q == 0, REST, SIB)
    swap = remote(
        crossed.at[jnp.where(half == 0, DOWN, before)], other_tile, x_send, x_recv, (o, mate)
    )
    swap.start()
    for m in range(1, NCH):
        far_wrap(m)
    k_rest = rows_dot(near_rows(OWN), near_rows(REST))
    bars = jnp.concatenate(
        [
            diag_weights(turned[0], UP, True),
            diag_weights(turned[1], DOWN, True),
            diag_weights(k_rest, REST),
        ],
        axis=1,
    )
    def trace_one():
        squares = [2.0 * folded(crossed[slot] * crossed[slot]) for slot in (before, DOWN)]
        squares.insert(0, folded(crossed[OWN] * crossed[OWN]))
        swap.wait()
        here = crossed[jnp.where(half == 0, before, DOWN)]
        product = 2.0 * folded(here * other_tile[...].T)
        squares[1] = squares[1] - jnp.where(half == 0, product, 0.0)
        squares[2] = squares[2] - jnp.where(half == 0, 0.0, product)
        one_out[...] = jnp.zeros((8, 128), F32)
        for k, slot in enumerate((OWN, before, DOWN)):
            one_out[k:k + 1, :] = jnp.sum(sums[slot] + squares[k], axis=0, keepdims=True)
        for copy in round_one:
            copy.start()

    def trace_two():
        total = one_out[...]
        for copy in round_one:
            copy.wait_recv()
        for r in range(7):
            total = total + tile_in[r]
        next_out[...] = total
        greeted(3)
        for copy in round_two:
            copy.start()

    round_one = [
        remote(one_out, tile_in.at[k], t_send.at[k], t_recv.at[k], (o, flipped(r)))
        for k, r in enumerate(range(1, 8))
    ]
    round_two = [
        remote(next_out, next_in.at[k], t_send.at[7 + k], t_recv.at[7 + k], (o, flipped(r)))
        for k, r in enumerate((8, 16, 24))
    ]

    trace_one()
    relay_far(0)
    add_density(bars, near_h.at[256:640], near_l.at[256:640])
    add_density(2.0 * crossed[OWN].T, far_h.at[0:ROWS], far_l.at[0:ROWS])

    own_pair = near_rows(OWN)
    trace_two()
    relay_far(1)
    for n in range(NCH):
        if 1 < n + 1 < NCH:
            relay_far(n + 1)
        start = n * CH
        wait_far(SIB, n)
        wait_far(REST, n)
        for at, slot in enumerate((SIB, UP, DOWN, REST)):
            h, l = halves(far[slot, pl.ds(start, CH), :])
            far_h[at * CH:(at + 1) * CH, :] = h
            far_l[at * CH:(at + 1) * CH, :] = l
        k_tile = rows_dot((far_h[...], far_l[...]), own_pair)
        bars = []
        side = far_row[start:start + CH, :]
        for at, slot in enumerate((SIB, UP, DOWN, REST)):
            gap = pair_energy(slot) - side - own_row[0:CH, :]
            amp = k_tile[at * CH:(at + 1) * CH, :] / gap
            bars.append(2.0 * amp - crossed[slot, pl.ds(start, CH), :])
        add_density(jnp.concatenate(bars, axis=0).T, far_h, far_l)

    for copy in round_one:
        copy.wait_send()

    for n in range(NCH):
        for flow in (S_SIB, S_PART, S_REST, S_FAR_UP, S_FAR_DOWN, S_FAR_SIB, S_FAR_REST):
            to_near(near_part(SIB, n), SIB, n, flow, (sibling, v)).wait_send()

        @pl.when(jnp.logical_not(last))
        def _():
            to_near(near_part(SIB, n), SIB, n, S_UP, (sibling, v)).wait_send()

        @pl.when(jnp.logical_not(first))
        def _():
            to_near(near_part(SIB, n), SIB, n, S_DOWN, (sibling, v)).wait_send()

        @pl.when(edge)
        def _():
            to_near(near_part(SIB, n), SIB, n, S_WRAP, (sibling, v)).wait_send()
            to_near(near_part(SIB, n), SIB, n, S_CROSS, (sibling, v)).wait_send()

    for copy in round_two:
        copy.wait()
    total = next_out[...]
    for k in range(3):
        total = total + next_in[k]
    summed = jnp.sum(total, axis=1, keepdims=True) / NVIR
    for k in range(3):
        trace[0:1, k:k + 1] = summed[k:k + 1, :]


def local(factor, occ_energy, vir_energy):
    vmem = pl.BlockSpec(memory_space=pltpu.VMEM)
    dma = pltpu.SemaphoreType.DMA
    block = (ROWS, NAUX)
    return pl.pallas_call(
        kernel,
        out_shape=(
            pltpu.VMEM((1,) + block, F32),
            jax.ShapeDtypeStruct((1, 3), F32),
        ),
        in_specs=[pl.BlockSpec(memory_space=pltpu.HBM), vmem, vmem],
        out_specs=(vmem, vmem),
        scratch_shapes=[
            pltpu.VMEM(block, F32),
            pltpu.VMEM((5,) + block, F32),
            pltpu.VMEM((5,) + block, F32),
            pltpu.VMEM(block, F32),
            pltpu.VMEM((5 * ROWS, NAUX), BF16),
            pltpu.VMEM((5 * ROWS, NAUX), BF16),
            pltpu.VMEM(block, BF16),
            pltpu.VMEM(block, BF16),
            pltpu.VMEM((5, ROWS, 128), F32),
            pltpu.VMEM((8, 128), F32),
            pltpu.VMEM((5, 8, 128), F32),
            pltpu.VMEM((5, 8, 128), F32),
            pltpu.VMEM((2, ROWS, 128), F32),
            pltpu.VMEM((ROWS, 128), F32),
            pltpu.VMEM((8, 128), F32),
            pltpu.VMEM((7, 8, 128), F32),
            pltpu.VMEM((8, 128), F32),
            pltpu.VMEM((3, 8, 128), F32),
            dma,
            dma((11, NCH)),
            dma((5, NCH)),
            dma((5, NCH)),
            dma((NCH,)),
            dma((5,)),
            dma((5,)),
            dma((10,)),
            dma((10,)),
            dma,
            dma,
            pltpu.SemaphoreType.REGULAR((4, 2)),
        ],
        compiler_params=pltpu.CompilerParams(
            collective_id=0, has_side_effects=True, vmem_limit_bytes=62 << 20
        ),
        cost_estimate=pl.CostEstimate(
            flops=6 * 24 * ROWS * ROWS * NAUX, bytes_accessed=2 * 4 * ROWS * NAUX, transcendentals=0
        ),
    )(factor, occ_energy.reshape(1, 1), vir_energy.reshape(1, 128))


def solution(mesh):
    placed = (P("occ", "vir", None), P("occ"), P("vir"))
    return jax.shard_map(
        local,
        mesh=mesh,
        in_specs=placed,
        out_specs=(P("occ", "vir", None), P("occ", None)),
        check_vma=False,
    )
```

```python
import jax
import jax.numpy as jnp
from jax import lax
from jax.experimental import pallas as pl
from jax.experimental.pallas import tpu as pltpu
from jax.sharding import PartitionSpec as P

NVIR = 4096
NAUX = 1280
ROWS = 128
NCH = 4
CH = ROWS // NCH
COLS = 256
MESH = pl.DeviceIdType.MESH
F32 = jnp.float32
BF16 = jnp.bfloat16

OWN, SIB, UP, DOWN, REST = range(5)
(
    S_SIB, S_UP, S_DOWN, S_PART, S_REST, S_FAR_UP, S_FAR_DOWN, S_FAR_SIB, S_FAR_REST,
    S_WRAP, S_CROSS,
) = range(11)


def halves(value):
    high = value.astype(BF16)
    return high, (value - high.astype(F32)).astype(BF16)


def rows_dot(former, latter):
    dims = (((1,), (1,)), ((), ()))

    def dot(a, b):
        return lax.dot_general(a, b, dims, preferred_element_type=F32)

    return dot(former[0], latter[0]) + (dot(former[0], latter[1]) + dot(former[1], latter[0]))


def folded(tile):
    return jnp.sum(tile.reshape(tile.shape[0] // 8, 8, 128), axis=0)


def kernel(
    factor, occ, vir, density, trace,
    own, near, far, staged, near_h, near_l, far_h, far_l, crossed, energy, energies, sums,
    turned, other_tile, one_out, tile_in, next_out, next_in,
    own_sem, send_sem, near_sem, far_sem, staged_sem, e_send, e_recv, t_send, t_recv,
    x_send, x_recv, entered,
):
    o = lax.axis_index("occ")
    v = lax.axis_index("vir")
    q = lax.rem(o, 2)
    x = lax.rem(o // 2, 4)
    y_lo = o // 8
    other_row = o + 8 - 16 * y_lo
    sibling = o + 1 - 2 * q
    mate = v + 1 - 2 * lax.rem(v, 2)
    first = x == 0
    last = x == 3
    edge = jnp.logical_or(first, last)
    inner = jnp.logical_not(edge)
    across = jnp.where(last, o - 6, o + 6)

    def occ_at(distance):
        return lax.rem(o + distance + 16, 16)

    up, down = occ_at(2), occ_at(-2)
    beyond = jnp.where(last, up, down)

    half = lax.rem(v, 2)
    z = v // 2
    below, above = z > 0, z < 15

    def flipped(r):
        out = v
        for bit in (1, 2, 4, 8, 16):
            if r & bit:
                out = out + bit - 2 * bit * lax.rem(v // bit, 2)
        return out

    own_copy = pltpu.make_async_copy(factor.at[0], own, own_sem)
    own_copy.start()

    barrier = pltpu.get_barrier_semaphore()
    peers = [(occ_at(d), v) for d in (1, -1, 2, -2)]
    peers += [(o, mate)]
    for peer in peers:
        pl.semaphore_signal(barrier, inc=1, device_id=peer, device_id_type=MESH)

    @pl.when(edge)
    def _():
        for peer in ((other_row, v), (across, v), (other_row, mate), (beyond, mate)):
            pl.semaphore_signal(barrier, inc=1, device_id=peer, device_id_type=MESH)

    @pl.when(below)
    def _():
        pl.semaphore_signal(barrier, inc=1, device_id=(o, v - 2), device_id_type=MESH)

    @pl.when(above)
    def _():
        pl.semaphore_signal(barrier, inc=1, device_id=(o, v + 2), device_id_type=MESH)

    energy[...] = jnp.zeros((8, 128), F32)
    energy[0:1, :] = vir[...]
    energy[1:2, :] = jnp.broadcast_to(occ[...], (1, 128))

    at_end = jnp.where(jnp.logical_and(below, above), 0, 1)
    pl.semaphore_wait(barrier, jnp.where(edge, len(peers) + 6, len(peers) + 2) - at_end)

    def remote(src, dst, send, recv, device):
        return pltpu.make_async_remote_copy(
            src_ref=src, dst_ref=dst, send_sem=send, recv_sem=recv,
            device_id=device, device_id_type=MESH,
        )

    def part(ref, n):
        return ref.at[pl.ds(n * CH, CH)]

    def mine(n):
        return own.at[pl.ds(n * CH, CH)]

    def to_near(src, slot, n, flow, device):
        return remote(
            src, near.at[slot, pl.ds(n * CH, CH)], send_sem.at[flow, n], near_sem.at[slot, n], device
        )

    def to_far(src, slot, n, flow, device):
        return remote(
            src, far.at[slot, pl.ds(n * CH, CH)], send_sem.at[flow, n], far_sem.at[slot, n], device
        )

    def to_staged(n):
        return remote(
            mine(n), part(staged, n), send_sem.at[S_PART, n], staged_sem.at[n], (other_row, v)
        )

    def near_part(slot, n):
        return near.at[slot, pl.ds(n * CH, CH)]

    def far_part(slot, n):
        return far.at[slot, pl.ds(n * CH, CH)]

    e_peers = [(occ_at(1), v), (occ_at(-1), v), (occ_at(2), v), (occ_at(-2), v), (o, mate)]
    e_copies = [
        remote(energy, energies.at[k], e_send.at[k], e_recv.at[k], peer)
        for k, peer in enumerate(e_peers)
    ]
    for copy in e_copies:
        copy.start()

    def far_wrap(n):
        @pl.when(last)
        def _():
            to_far(mine(n), DOWN, n, S_FAR_UP, (up, mate)).start()

        @pl.when(first)
        def _():
            to_far(mine(n), UP, n, S_FAR_DOWN, (down, mate)).start()

    own_copy.wait()
    for n in range(NCH):
        @pl.when(edge)
        def _():
            to_staged(n).start()

        if n == 0:
            far_wrap(0)

        @pl.when(inner)
        def _():
            to_far(mine(n), 0, n, S_PART, (o, mate)).start()

        @pl.when(jnp.logical_not(last))
        def _():
            to_near(mine(n), DOWN, n, S_UP, (up, v)).start()

        @pl.when(jnp.logical_not(first))
        def _():
            to_near(mine(n), UP, n, S_DOWN, (down, v)).start()

        to_near(mine(n), SIB, n, S_SIB, (sibling, v)).start()

    def wait_near(slot, n):
        to_near(near_part(slot, n), slot, n, S_SIB, (sibling, v)).wait_recv()

    def wait_far(slot, n):
        to_far(far_part(slot, n), slot, n, S_SIB, (sibling, v)).wait_recv()

    def relay_staged(n):
        @pl.when(edge)
        def _():
            to_staged(n).wait_recv()
            to_near(part(staged, n), jnp.where(last, DOWN, UP), n, S_WRAP, (across, v)).start()
            to_far(part(staged, n), 0, n, S_CROSS, (other_row, mate)).start()

    def take_partner(n):
        wait_far(0, n)
        to_far(far_part(0, n), SIB, n, S_FAR_SIB, (sibling, v)).start()

    def relay_partner(n):
        @pl.when(jnp.logical_not(last))
        def _():
            to_far(far_part(0, n), DOWN, n, S_FAR_UP, (up, v)).start()

        @pl.when(jnp.logical_not(first))
        def _():
            to_far(far_part(0, n), UP, n, S_FAR_DOWN, (down, v)).start()

    passed = jnp.where(q == 0, UP, DOWN)

    def relay_near(n):
        wait_near(UP, n)
        wait_near(DOWN, n)
        to_near(near_part(passed, n), REST, n, S_REST, (sibling, v)).start()

    def relay_far(n):
        wait_far(UP, n)
        wait_far(DOWN, n)
        to_far(far_part(passed, n), REST, n, S_FAR_REST, (sibling, v)).start()

    def split_near(slot, start, count):
        rows = pl.ds(slot * ROWS + start, count)
        h, l = halves(near[slot, pl.ds(start, count), :])
        near_h[rows, :] = h
        near_l[rows, :] = l

    def split_far(slot, start, count):
        rows = pl.ds(slot * ROWS + start, count)
        h, l = halves(far[slot, pl.ds(start, count), :])
        far_h[rows, :] = h
        far_l[rows, :] = l

    def near_rows(slot, count=1):
        rows = pl.ds(slot * ROWS, count * ROWS)
        return near_h[rows, :], near_l[rows, :]

    def add_density(weights, latter_h, latter_l, fresh=False):
        w_h, w_l = halves(weights)
        for c in range(NAUX // COLS):
            cols = pl.ds(c * COLS, COLS)
            h, l = latter_h[:, cols], latter_l[:, cols]
            term = (
                jnp.dot(w_h, h, preferred_element_type=F32)
                + jnp.dot(w_h, l, preferred_element_type=F32)
                + jnp.dot(w_l, h, preferred_element_type=F32)
            )
            density[0, :, cols] = term if fresh else density[0, :, cols] + term

    def pair_energy(slot):
        if slot == OWN:
            row = energy[1:2, :]
        elif slot == UP:
            row = energies[3, 1:2, :]
        elif slot == DOWN:
            row = energies[2, 1:2, :]
        elif slot == SIB:
            row = jnp.where(q == 0, energies[1, 1:2, :], energies[0, 1:2, :])
        else:
            row = jnp.where(q == 0, energies[0, 1:2, :], energies[1, 1:2, :])
        return row + energy[1:2, :]

    def diag_weights(k_tile, slot, turned=False):
        across_b = jnp.broadcast_to(energy[0:1, :], (ROWS, 128))
        gap = pair_energy(slot) - across_b.T - across_b
        amp = k_tile / gap
        bar = 2.0 * amp.T - amp if turned else 2.0 * amp - amp.T
        sums[slot] = folded((amp.T if turned else amp) * bar)
        return 2.0 * bar if slot == OWN else bar

    def greet(step):
        @pl.when(z >= 1 << step)
        def _():
            pl.semaphore_signal(
                entered.at[step, 0], inc=1, device_id=(o, v - (2 << step)), device_id_type=MESH
            )

        @pl.when(z < 16 - (1 << step))
        def _():
            pl.semaphore_signal(
                entered.at[step, 1], inc=1, device_id=(o, v + (2 << step)), device_id_type=MESH
            )

    def greeted(step):
        @pl.when(z < 16 - (1 << step))
        def _():
            pl.semaphore_wait(entered.at[step, 0], 1)

        @pl.when(z >= 1 << step)
        def _():
            pl.semaphore_wait(entered.at[step, 1], 1)

    greet(0)
    relay_staged(0)
    h, l = halves(own[...])
    near_h[0:ROWS, :] = h
    near_l[0:ROWS, :] = l
    for copy in e_copies:
        copy.wait()
    for n in range(NCH):
        wait_near(SIB, n)
    split_near(SIB, 0, ROWS)
    k_first = rows_dot(near_rows(OWN), near_rows(OWN, 2))
    bars = jnp.concatenate(
        [diag_weights(k_first[:, :128], OWN), diag_weights(k_first[:, 128:], SIB)], axis=1
    )
    add_density(bars, near_h.at[0:256], near_l.at[0:256], fresh=True)

    far_row = jnp.broadcast_to(energies[4, 0:1, :], (ROWS, 128)).T
    own_row = jnp.broadcast_to(energy[0:1, :], (ROWS, 128))
    for n in range(1, NCH + 1):
        if n < NCH:
            relay_staged(n)
        take_partner(n - 1)
        relay_near(n - 1)
        relay_partner(n - 1)
        if n == 1:
            greeted(0)
            greet(1)
        elif n == 2:
            greeted(1)
            greet(2)
        elif n == 3:
            greeted(2)
            greet(3)
        start = (n - 1) * CH
        split_far(0, start, CH)
        split_near(UP, start, CH)
        split_near(DOWN, start, CH)
        lot = [
            jnp.concatenate(
                [near[UP * ROWS + start:UP * ROWS + start + CH, :],
                 near[DOWN * ROWS + start:DOWN * ROWS + start + CH, :],
                 far[start:start + CH, :]],
                axis=0,
            )
            for near, far in ((near_h, far_h), (near_l, far_l))
        ]
        k_lot = rows_dot(lot, near_rows(OWN, 2))
        turned[0, start:start + CH, :] = k_lot[0:CH, :128]
        turned[1, start:start + CH, :] = k_lot[CH:2 * CH, :128]
        for slot in (OWN, SIB):
            gap = pair_energy(slot) - far_row[start:start + CH, :] - own_row[0:CH, :]
            crossed[slot, start:start + CH, :] = k_lot[2 * CH:, slot * 128:(slot + 1) * 128] / gap

    for n in range(NCH):
        wait_near(REST, n)
    split_near(REST, 0, ROWS)

    k_cross = rows_dot((far_h[0:ROWS, :], far_l[0:ROWS, :]), near_rows(UP, 3))
    for at, slot in enumerate((UP, DOWN, REST)):
        crossed[slot] = k_cross[:, at * 128:(at + 1) * 128] / (pair_energy(slot) - far_row - own_row)

    before = jnp.where(q == 0, REST, SIB)
    swap = remote(
        crossed.at[jnp.where(half == 0, DOWN, before)], other_tile, x_send, x_recv, (o, mate)
    )
    swap.start()
    for m in range(1, NCH):
        far_wrap(m)
    k_rest = rows_dot(near_rows(OWN), near_rows(REST))
    bars = jnp.concatenate(
        [
            diag_weights(turned[0], UP, True),
            diag_weights(turned[1], DOWN, True),
            diag_weights(k_rest, REST),
        ],
        axis=1,
    )
    def trace_one():
        squares = [2.0 * folded(crossed[slot] * crossed[slot]) for slot in (before, DOWN)]
        squares.insert(0, folded(crossed[OWN] * crossed[OWN]))
        swap.wait()
        here = crossed[jnp.where(half == 0, before, DOWN)]
        product = 2.0 * folded(here * other_tile[...].T)
        squares[1] = squares[1] - jnp.where(half == 0, product, 0.0)
        squares[2] = squares[2] - jnp.where(half == 0, 0.0, product)
        one_out[...] = jnp.zeros((8, 128), F32)
        for k, slot in enumerate((OWN, before, DOWN)):
            one_out[k:k + 1, :] = jnp.sum(sums[slot] + squares[k], axis=0, keepdims=True)
        for copy in round_one:
            copy.start()

    def trace_two():
        total = one_out[...]
        for copy in round_one:
            copy.wait_recv()
        for r in range(7):
            total = total + tile_in[r]
        next_out[...] = total
        greeted(3)
        for copy in round_two:
            copy.start()

    round_one = [
        remote(one_out, tile_in.at[k], t_send.at[k], t_recv.at[k], (o, flipped(r)))
        for k, r in enumerate(range(1, 8))
    ]
    round_two = [
        remote(next_out, next_in.at[k], t_send.at[7 + k], t_recv.at[7 + k], (o, flipped(r)))
        for k, r in enumerate((8, 16, 24))
    ]

    add_density(bars, near_h.at[256:640], near_l.at[256:640])
    trace_one()
    relay_far(0)
    add_density(2.0 * crossed[OWN].T, far_h.at[0:ROWS], far_l.at[0:ROWS])

    own_pair = near_rows(OWN)
    trace_two()
    relay_far(1)
    for n in range(NCH):
        if 1 < n + 1 < NCH:
            relay_far(n + 1)
        start = n * CH
        wait_far(SIB, n)
        wait_far(REST, n)
        for at, slot in enumerate((SIB, UP, DOWN, REST)):
            h, l = halves(far[slot, pl.ds(start, CH), :])
            far_h[at * CH:(at + 1) * CH, :] = h
            far_l[at * CH:(at + 1) * CH, :] = l
        k_tile = rows_dot((far_h[...], far_l[...]), own_pair)
        bars = []
        side = far_row[start:start + CH, :]
        for at, slot in enumerate((SIB, UP, DOWN, REST)):
            gap = pair_energy(slot) - side - own_row[0:CH, :]
            amp = k_tile[at * CH:(at + 1) * CH, :] / gap
            bars.append(2.0 * amp - crossed[slot, pl.ds(start, CH), :])
        add_density(jnp.concatenate(bars, axis=0).T, far_h, far_l)

    for copy in round_one:
        copy.wait_send()

    for n in range(NCH):
        for flow in (S_SIB, S_PART, S_REST, S_FAR_UP, S_FAR_DOWN, S_FAR_SIB, S_FAR_REST):
            to_near(near_part(SIB, n), SIB, n, flow, (sibling, v)).wait_send()

        @pl.when(jnp.logical_not(last))
        def _():
            to_near(near_part(SIB, n), SIB, n, S_UP, (sibling, v)).wait_send()

        @pl.when(jnp.logical_not(first))
        def _():
            to_near(near_part(SIB, n), SIB, n, S_DOWN, (sibling, v)).wait_send()

        @pl.when(edge)
        def _():
            to_near(near_part(SIB, n), SIB, n, S_WRAP, (sibling, v)).wait_send()
            to_near(near_part(SIB, n), SIB, n, S_CROSS, (sibling, v)).wait_send()

    for copy in round_two:
        copy.wait()
    total = next_out[...]
    for k in range(3):
        total = total + next_in[k]
    summed = jnp.sum(total, axis=1, keepdims=True) / NVIR
    for k in range(3):
        trace[0:1, k:k + 1] = summed[k:k + 1, :]


def local(factor, occ_energy, vir_energy):
    vmem = pl.BlockSpec(memory_space=pltpu.VMEM)
    dma = pltpu.SemaphoreType.DMA
    block = (ROWS, NAUX)
    return pl.pallas_call(
        kernel,
        out_shape=(
            pltpu.VMEM((1,) + block, F32),
            pltpu.VMEM((1, 3), F32),
        ),
        in_specs=[pl.BlockSpec(memory_space=pltpu.HBM), vmem, vmem],
        out_specs=(vmem, vmem),
        scratch_shapes=[
            pltpu.VMEM(block, F32),
            pltpu.VMEM((5,) + block, F32),
            pltpu.VMEM((5,) + block, F32),
            pltpu.VMEM(block, F32),
            pltpu.VMEM((5 * ROWS, NAUX), BF16),
            pltpu.VMEM((5 * ROWS, NAUX), BF16),
            pltpu.VMEM(block, BF16),
            pltpu.VMEM(block, BF16),
            pltpu.VMEM((5, ROWS, 128), F32),
            pltpu.VMEM((8, 128), F32),
            pltpu.VMEM((5, 8, 128), F32),
            pltpu.VMEM((5, 8, 128), F32),
            pltpu.VMEM((2, ROWS, 128), F32),
            pltpu.VMEM((ROWS, 128), F32),
            pltpu.VMEM((8, 128), F32),
            pltpu.VMEM((7, 8, 128), F32),
            pltpu.VMEM((8, 128), F32),
            pltpu.VMEM((3, 8, 128), F32),
            dma,
            dma((11, NCH)),
            dma((5, NCH)),
            dma((5, NCH)),
            dma((NCH,)),
            dma((5,)),
            dma((5,)),
            dma((10,)),
            dma((10,)),
            dma,
            dma,
            pltpu.SemaphoreType.REGULAR((4, 2)),
        ],
        compiler_params=pltpu.CompilerParams(
            collective_id=0, has_side_effects=True, vmem_limit_bytes=62 << 20
        ),
        cost_estimate=pl.CostEstimate(
            flops=6 * 24 * ROWS * ROWS * NAUX, bytes_accessed=2 * 4 * ROWS * NAUX, transcendentals=0
        ),
    )(factor, occ_energy.reshape(1, 1), vir_energy.reshape(1, 128))


def solution(mesh):
    placed = (P("occ", "vir", None), P("occ"), P("vir"))
    return jax.shard_map(
        local,
        mesh=mesh,
        in_specs=placed,
        out_specs=(P("occ", "vir", None), P("occ", None)),
        check_vma=False,
    )
```
